32 devices in a mesh: row: 8 (over y, x, core), ctr: 4 (over z).
Axes of the slice: x: 2, y: 2, z: 4, core: 2. Of those that a mesh axis runs over, the one named last changes fastest.
Arguments:
- left_factor: bfloat16 [32, 1024, 1024], P('row', None, 'ctr'), may hold values from -6 to 6
- left_inner: bfloat16 [32, 1024, 1024], P('row', None, 'ctr'), may hold values from -0.1875 to 0.1875
- right_inner: bfloat16 [1024, 1024], P('row', 'ctr'), may hold values from -6 to 6
- right_outer: bfloat16 [1024, 1024], P('row', 'ctr'), may hold values from -0.03125 to 0.03125
- pattern: int32 [32, 32], P('row', 'ctr'), may hold values from 0 to 1, as said below
- start_matrix: int32 [1024, 32], replicated, may hold values from -4 to 4
Outputs:
- compressed_left: bfloat16 [32, 1024, 32], P('row')
- compressed_right: bfloat16 [32, 1024, 32], P('row')
The draws below stay inside these ranges and needn't reach their ends.
Inputs may be any that keep to these rules, and one draw needn't show every extreme that they name: `pattern`: in every tile row at least one of each aligned group of four contraction tiles is kept; how many are kept differs from row to row.
All inputs are finite; a program needn't handle non-finite values.
Results may differ from the reference program's by a relative error of at most 0.025.
Values may be sent and summed in bfloat16 or wider, within the bound.
A program may use at most 64 MiB of HBM per device.

```python
import math
import jax
import jax.numpy as jnp
from jax import lax

TILE = 1024
RANK = 32
STEPS = 2
ROWS_T = 32
CTR_T = 32


def draw_pattern(key, part):
    first_key, second_key, third_key = jax.random.split(key, 3)
    levels = jax.random.randint(first_key, (ROWS_T, 1), 1, 9)
    throws = jax.random.randint(second_key, (ROWS_T, CTR_T), 0, 8)
    offset = jax.random.randint(third_key, (ROWS_T, 1), 0, 4)
    column = jnp.arange(CTR_T, dtype=jnp.int32)[None, :] % 4
    return jnp.where((throws < levels) | (column == offset), 1, 0).astype(jnp.int32)


def with_ends(result, own_key, least, high):
    longest = result.shape.index(max(result.shape))
    spots = []
    for shift in (0, 1):
        where = [jax.random.randint(jax.random.fold_in(own_key, axis), (), 0, length) for axis, length in enumerate(result.shape)]
        where[longest] = (where[longest] + shift) % result.shape[longest]
        spots.append(tuple(where))
    return result.at[spots[0]].set(least).at[spots[1]].set(high)


def level_of(own_key, shape, shards, least, largest):
    loudness = 1.0
    for axis_at, shards_of in shards:
        steps = jax.random.uniform(jax.random.fold_in(jax.random.fold_in(own_key, 6), axis_at), (shards_of,), jnp.float32, least / len(shards), largest / len(shards))
        loudness = loudness * jnp.repeat(jnp.exp(steps), shape[axis_at] // shards_of).reshape((-1,) + (1,) * (len(shape) - 1 - axis_at))
    return loudness


def bell_draw(key, shape, deviation, bound, cuts=(), kind=jnp.bfloat16):
    values = deviation * jax.random.normal(key, shape, jnp.float32)
    if cuts:
        values = values * level_of(key, shape, cuts, -0.22, 0.18)
    return jnp.clip(values, -bound, bound).astype(kind)


def setup_inputs(seed: int = 0) -> dict:
    streams_of = jax.random.split(jax.random.key(seed), 7)
    return {
        "left_factor": bell_draw(streams_of[0], (ROWS_T, TILE, CTR_T * RANK), 1.0, 6.0, ((0, 8), (2, 4))),
        "left_inner": bell_draw(streams_of[1], (ROWS_T, TILE, CTR_T * RANK), TILE ** -0.5, 0.1875, ((0, 8), (2, 4))),
        "right_inner": bell_draw(streams_of[2], (TILE, CTR_T * RANK), 1.0, 6.0, ((0, 8), (1, 4))),
        "right_outer": bell_draw(streams_of[3], (TILE, CTR_T * RANK), (RANK * RANK * CTR_T) ** -0.5, 0.03125, ((0, 8), (1, 4))),
        "pattern": draw_pattern(jax.random.fold_in(streams_of[6], 71), 0),
        "start_matrix": with_ends(jax.random.randint(streams_of[5], (TILE, RANK), -4, 5), jax.random.fold_in(streams_of[5], 1), -4, 4).astype(jnp.int32),
    }


highest = lax.Precision.HIGHEST

def forward_apply(factor, inner_block, outer_stack, vectors):
    shrunk = jnp.dot(outer_stack.T.astype(jnp.float32), vectors.astype(jnp.float32), preferred_element_type=jnp.float32).reshape(CTR_T, RANK, RANK)
    mapped = jnp.einsum('krs,ksq->krq', inner_block, shrunk, precision=highest)
    mapped = mapped.astype(jnp.bfloat16).reshape(CTR_T * RANK, RANK)
    return jnp.dot(factor.astype(jnp.float32), mapped.astype(jnp.float32), preferred_element_type=jnp.float32)

def adjoint_apply(factor, inner_block, outer_stack, vectors):
    shrunk = jnp.dot(factor.T.astype(jnp.float32), vectors.astype(jnp.float32), preferred_element_type=jnp.float32).reshape(CTR_T, RANK, RANK)
    mapped = jnp.einsum('krs,krq->ksq', inner_block, shrunk, precision=highest)
    mapped = mapped.astype(jnp.bfloat16).reshape(CTR_T * RANK, RANK)
    return jnp.dot(outer_stack.astype(jnp.float32), mapped.astype(jnp.float32), preferred_element_type=jnp.float32)

def orthonormal(panel):
    gram_matrix = jnp.dot(panel.T.astype(jnp.float32), panel.astype(jnp.float32), precision=highest, preferred_element_type=jnp.float32)
    factor_low = jnp.linalg.cholesky(gram_matrix)
    return lax.linalg.triangular_solve(factor_low, panel, left_side=False, lower=True, transpose_a=True)

def reference(left_factor, left_inner, right_inner, right_outer, pattern, start_matrix):
    start_bf = start_matrix.astype(jnp.bfloat16)
    inner_right = right_inner.astype(jnp.float32).reshape(TILE, CTR_T, RANK)

    def per_row(row_items):
        factor, inner_rows, pattern_row = row_items
        coupled = jnp.einsum('tkr,tks->krs', inner_rows.astype(jnp.float32).reshape(TILE, CTR_T, RANK), inner_right, precision=highest)
        coupled = (coupled * pattern_row.astype(jnp.float32)[:, None, None]).astype(jnp.bfloat16)
        inner_block = lax.optimization_barrier(coupled).astype(jnp.float32)
        basis_now = orthonormal(forward_apply(factor, inner_block, right_outer, start_bf))
        for sweep_index in range(STEPS):
            dual_basis = orthonormal(adjoint_apply(factor, inner_block, right_outer, basis_now.astype(jnp.bfloat16)))
            basis_now = orthonormal(forward_apply(factor, inner_block, right_outer, dual_basis.astype(jnp.bfloat16)))
        weights = adjoint_apply(factor, inner_block, right_outer, basis_now.astype(jnp.bfloat16))
        return ((math.sqrt(TILE) * basis_now).astype(jnp.bfloat16), weights.astype(jnp.bfloat16))
    return lax.map(per_row, (left_factor, left_inner, pattern))
```

```python
import functools
import math

import jax
import jax.numpy as jnp
from jax import lax
from jax.experimental import pallas as pl
from jax.experimental.pallas import tpu as pltpu
from jax.sharding import PartitionSpec as P

STEPS = 2


highest = lax.Precision.HIGHEST


def gram_of(panel):
    return jnp.einsum(
        "itr,its->irs", panel, panel, precision=highest, preferred_element_type=jnp.float32
    )


def solve_rows(gram_matrix, panel):
    factor_low = jnp.linalg.cholesky(gram_matrix)
    return lax.linalg.triangular_solve(
        factor_low, panel, left_side=False, lower=True, transpose_a=True
    )


def reduced_basis(partial_value):
    summed = lax.psum(partial_value.astype(jnp.bfloat16), "ctr").astype(jnp.float32)
    return solve_rows(gram_of(summed), summed).astype(jnp.bfloat16)


def reduced_weights(partial_value):
    return lax.psum(partial_value.astype(jnp.bfloat16), "ctr")


def local_any(left_factor, left_inner, right_inner, right_outer, pattern, start_matrix):
    rows_here = left_factor.shape[0]
    tile_len = left_factor.shape[1]
    columns_here = left_factor.shape[2]
    rank_len = start_matrix.shape[1]
    blocks = columns_here // rank_len
    inner_piece = lax.all_gather(right_inner, "row", axis=0, tiled=True)
    outer_piece = lax.all_gather(right_outer, "row", axis=0, tiled=True)
    taken = inner_piece.shape[0]
    coupled = jnp.einsum(
        "itkr,tks->ikrs",
        left_inner.reshape(rows_here, taken, blocks, rank_len),
        inner_piece.reshape(taken, blocks, rank_len),
        preferred_element_type=jnp.float32,
    )
    coupled, outer_full = (coupled, outer_piece)
    coupled = (coupled * pattern.astype(jnp.float32)[:, :, None, None]).astype(jnp.bfloat16)
    inner_block = lax.optimization_barrier(coupled).astype(jnp.float32)

    def forward(vectors):
        shrunk = jnp.einsum(
            "tc,itq->icq", outer_full, vectors, preferred_element_type=jnp.float32
        ).reshape(rows_here, blocks, rank_len, rank_len)
        mapped = jnp.einsum("ikrs,iksq->ikrq", inner_block, shrunk, precision=highest)
        mapped = mapped.astype(jnp.bfloat16).reshape(rows_here, columns_here, rank_len)
        return jnp.einsum("itc,icq->itq", left_factor, mapped, preferred_element_type=jnp.float32)

    def adjoint(vectors):
        shrunk = jnp.einsum(
            "itc,itq->icq", left_factor, vectors, preferred_element_type=jnp.float32
        ).reshape(rows_here, blocks, rank_len, rank_len)
        mapped = jnp.einsum("ikrs,ikrq->iksq", inner_block, shrunk, precision=highest)
        mapped = mapped.astype(jnp.bfloat16).reshape(rows_here, columns_here, rank_len)
        return jnp.einsum("tc,icq->itq", outer_full, mapped, preferred_element_type=jnp.float32)

    start_bf = jnp.broadcast_to(
        start_matrix.astype(jnp.bfloat16)[None], (rows_here, tile_len, rank_len)
    )
    basis_now = reduced_basis(forward(start_bf))
    for sweep_index in range(STEPS):
        dual_basis = reduced_basis(adjoint(basis_now))
        basis_now = reduced_basis(forward(dual_basis))
    weights = reduced_weights(adjoint(basis_now))
    compressed_left = (basis_now.astype(jnp.float32) * math.sqrt(tile_len)).astype(jnp.bfloat16)
    return (compressed_left, weights)


F32 = jnp.float32
BF16 = jnp.bfloat16


def nn(a, b):
    return lax.dot_general(a, b, (((1,), (0,)), ((), ())), preferred_element_type=F32)


def nt(a, b):
    return lax.dot_general(a, b, (((1,), (1,)), ((), ())), preferred_element_type=F32)


def inverse_factor(gram):
    n = gram.shape[0]
    row_at = lax.broadcasted_iota(jnp.int32, (n, n), 0)
    col_at = lax.broadcasted_iota(jnp.int32, (n, n), 1)
    rest = gram
    inverse = jnp.where(row_at == col_at, 1.0, 0.0).astype(F32)
    for j in range(n - 1):
        ratio = rest[:, j : j + 1] / rest[j : j + 1, j : j + 1]
        ratio = jnp.where(row_at > j, ratio, 0.0)
        rest = rest - ratio * rest[j : j + 1, :]
        inverse = inverse - ratio * inverse[j : j + 1, :]
    pivots = jnp.sum(jnp.where(row_at == col_at, rest, 0.0), axis=1, keepdims=True)
    return inverse * lax.rsqrt(pivots)


def orth_rows(panel):
    high = panel.astype(BF16)
    inverse = inverse_factor(nt(high, high))
    inverse_high = inverse.astype(BF16)
    inverse_low = (inverse - inverse_high.astype(F32)).astype(BF16)
    return nn(inverse_high, high) + nn(inverse_low, high)


def kernel(
    n_row, n_ctr, chunks,
    u_hbm, v_hbm, x_ref, y_ref, pattern_ref, start_ref,
    left_ref, right_ref,
    u_all, v_all, x_all, y_all, yb_all, c_all, z_ref, couple_out, couple_in,
    local_sem, u_send, u_recv, x_send, x_recv, yz_send, yz_recv, yr_send, yr_recv,
    k_send, k_recv, l_send, l_recv, r_send, r_recv,
):
    me_r, me_c = lax.axis_index("row"), lax.axis_index("ctr")
    tile = u_hbm.shape[1]
    cols = u_hbm.shape[2]
    part = x_ref.shape[0]
    rank = start_ref.shape[0]
    blocks = pattern_ref.shape[1]
    step = tile // chunks
    z_peers = [lax.rem(me_c + d, n_ctr) for d in range(n_ctr)]
    r_peers = [lax.rem(me_r + d, n_row) for d in range(n_row)]
    mine = pl.ds(pl.multiple_of(me_r * part, part), part)

    def remote(src, dst, send, recv, where):
        return pltpu.make_async_remote_copy(
            src_ref=src, dst_ref=dst, send_sem=send, recv_sem=recv,
            device_id=where, device_id_type=pl.DeviceIdType.MESH,
        )

    v_copy = pltpu.make_async_copy(v_hbm, v_all, local_sem.at[0])
    v_copy.start()
    own_u = pltpu.make_async_copy(u_hbm.at[me_c], u_all.at[:, pl.ds(0, cols)], local_sem.at[1])
    own_u.start()

    barrier = pltpu.get_barrier_semaphore()
    for d in range(1, n_ctr):
        pl.semaphore_signal(barrier, inc=1, device_id={"ctr": z_peers[d]}, device_id_type=pl.DeviceIdType.MESH)
    for d in range(1, n_row):
        pl.semaphore_signal(barrier, inc=1, device_id={"row": r_peers[d]}, device_id_type=pl.DeviceIdType.MESH)
    pl.semaphore_wait(barrier, n_ctr + n_row - 2)

    yz = [None] + [
        remote(y_ref, y_all.at[mine, pl.ds(d * cols, cols)], yz_send.at[d], yz_recv.at[d], {"ctr": z_peers[d]})
        for d in range(1, n_ctr)
    ]
    xs = [None] + [
        remote(x_ref, x_all.at[mine, :], x_send.at[d], x_recv.at[d], {"row": r_peers[d]})
        for d in range(1, n_row)
    ]
    for copy in yz[1:] + xs[1:]:
        copy.start()
    us = {}
    for chunk in range(chunks):
        rows = pl.ds(chunk * step, step)
        for d in range(1, n_ctr):
            us[chunk, d] = remote(
                u_hbm.at[z_peers[d], rows, :], u_all.at[rows, pl.ds(d * cols, cols)],
                u_send.at[chunk, d], u_recv.at[chunk, d], {"ctr": z_peers[d]},
            )
            us[chunk, d].start()
    x_all[mine, :] = x_ref[...]
    y_all[mine, pl.ds(0, cols)] = y_ref[...]
    yr = {}
    for k in range(n_ctr):
        if k:
            yz[k].wait_recv()
        for d in range(1, n_row):
            place = y_all.at[mine, pl.ds(k * cols, cols)]
            yr[k, d] = remote(
                place, place, yr_send.at[k, d], yr_recv.at[k, d], {"row": r_peers[d]}
            )
            yr[k, d].start()

    row_at = lax.broadcasted_iota(jnp.int32, (cols, cols), 0)
    col_at = lax.broadcasted_iota(jnp.int32, (cols, cols), 1)
    diagonal = jnp.where(row_at // rank == col_at // rank, 1.0, 0.0).astype(F32)
    fold = jnp.where(
        lax.broadcasted_iota(jnp.int32, (rank, cols), 1) % rank
        == lax.broadcasted_iota(jnp.int32, (rank, cols), 0), 1.0, 0.0
    ).astype(BF16)
    unfold = jnp.where(
        lax.broadcasted_iota(jnp.int32, (cols, rank), 0) % rank
        == lax.broadcasted_iota(jnp.int32, (cols, rank), 1), 1.0, 0.0
    ).astype(BF16)
    spread = jnp.where(
        lax.broadcasted_iota(jnp.int32, (blocks, cols), 1) // rank
        == lax.broadcasted_iota(jnp.int32, (blocks, cols), 0), 1.0, 0.0
    ).astype(F32)
    v_copy.wait()
    for d in range(1, n_row):
        xs[d].wait_recv()
    x_turned = x_all[...].T
    couples = [None]
    for d in range(n_ctr):
        kept = pattern_ref[pl.ds(z_peers[d], 1), :].astype(F32)
        kept = nn(jnp.broadcast_to(kept, (8, blocks)).astype(BF16), spread.astype(BF16))[0:1, :]
        product = nn(x_turned, v_all[z_peers[d]])
        product = (product * diagonal * kept).astype(BF16)
        compact = nn(fold, product).astype(BF16)
        if d:
            couple_out[d] = compact
            copy = remote(couple_out.at[d], couple_in.at[d], k_send.at[d], k_recv.at[d], {"ctr": z_peers[d]})
            copy.start()
            couples.append(copy)
        else:
            couple_in[0] = compact

    for k in range(n_ctr):
        for d in range(1, n_row):
            yr[k, d].wait_recv()
        if k:
            couples[k].wait_recv()
        wide = (nn(unfold, couple_in[k]) * diagonal).astype(BF16)
        at = pl.ds(k * cols, cols)
        yb_all[:, at] = nn(y_all[:, at], wide).astype(BF16)

    own_u.wait()
    start = start_ref[...].astype(F32).astype(BF16)
    for chunk in range(chunks):
        rows = pl.ds(chunk * step, step)
        for d in range(1, n_ctr):
            us[chunk, d].wait_recv()
        c_all[rows, :] = nt(u_all[rows, :], yb_all[...]).astype(BF16)
        z_ref[:, rows] = nt(start, c_all[rows, :])

    basis = orth_rows(z_ref[...])
    for sweep_index in range(STEPS):
        dual = orth_rows(nn(basis.astype(BF16), c_all[...]))
        basis = orth_rows(nt(dual.astype(BF16), c_all[...]))

    def share(ref, value, send, recv):
        ref[me_c] = value
        copies = [
            remote(ref.at[me_c], ref.at[me_c], send.at[d], recv.at[d], {"ctr": z_peers[d]})
            for d in range(1, n_ctr)
        ]
        for copy in copies:
            copy.start()
        return copies

    left = share(left_ref, (basis * math.sqrt(tile)).astype(BF16), l_send, l_recv)
    right = share(right_ref, nn(basis.astype(BF16), c_all[...]).astype(BF16), r_send, r_recv)
    for copy in yz[1:] + xs[1:] + list(us.values()) + list(yr.values()) + couples[1:]:
        copy.wait_send()
    for copy in left + right:
        copy.wait()


def local_tile(n_row, n_ctr, left_factor, left_inner, right_inner, right_outer, pattern, start_matrix):
    rows_here, tile, cols = left_factor.shape
    rank = start_matrix.shape[1]
    chunks = 4
    dma = lambda *shape: pltpu.SemaphoreType.DMA(shape)
    vmem = pl.BlockSpec(memory_space=pltpu.VMEM)
    hbm = pl.BlockSpec(memory_space=pl.ANY)
    width = n_ctr * cols
    turned = jax.ShapeDtypeStruct((rows_here, rank, tile), BF16)
    left, right = pl.pallas_call(
        functools.partial(kernel, n_row, n_ctr, chunks),
        out_shape=(turned, turned),
        in_specs=[hbm, hbm, vmem, vmem, vmem, vmem],
        out_specs=(vmem, vmem),
        scratch_shapes=[
            pltpu.VMEM((tile, width), BF16),
            pltpu.VMEM((rows_here, tile, cols), BF16),
            pltpu.VMEM((tile, cols), BF16),
            pltpu.VMEM((tile, width), BF16),
            pltpu.VMEM((tile, width), BF16),
            pltpu.VMEM((tile, tile), BF16),
            pltpu.VMEM((rank, tile), F32),
            pltpu.VMEM((n_ctr, rank, cols), BF16),
            pltpu.VMEM((n_ctr, rank, cols), BF16),
            dma(2),
            dma(chunks, n_ctr), dma(chunks, n_ctr),
            dma(n_row), dma(n_row),
            dma(n_ctr), dma(n_ctr),
            dma(n_ctr, n_row), dma(n_ctr, n_row),
            dma(n_ctr), dma(n_ctr),
            dma(n_ctr), dma(n_ctr),
            dma(n_ctr), dma(n_ctr),
        ],
        compiler_params=pltpu.CompilerParams(
            collective_id=0, has_side_effects=True, vmem_limit_bytes=48 * 1024 * 1024
        ),
    )(left_factor, left_inner, right_inner, right_outer, pattern, start_matrix.T)
    return left.transpose(0, 2, 1), right.transpose(0, 2, 1)


def solution(mesh):
    n_row, n_ctr = mesh.shape["row"], mesh.shape["ctr"]

    def local(left_factor, *others):
        if left_factor.shape[0] == n_ctr:
            return local_tile(n_row, n_ctr, left_factor, *others)
        return local_any(left_factor, *others)

    return jax.shard_map(
        local,
        mesh=mesh,
        in_specs=(
            P("row", None, "ctr"),
            P("row", None, "ctr"),
            P("row", "ctr"),
            P("row", "ctr"),
            P("row", "ctr"),
            P(),
        ),
        out_specs=(P("row", None, None), P("row", None, None)),
        check_vma=False,
    )
```

```python
import functools
import math

import jax
import jax.numpy as jnp
from jax import lax
from jax.experimental import pallas as pl
from jax.experimental.pallas import tpu as pltpu
from jax.sharding import PartitionSpec as P

STEPS = 2


highest = lax.Precision.HIGHEST


def gram_of(panel):
    return jnp.einsum(
        "itr,its->irs", panel, panel, precision=highest, preferred_element_type=jnp.float32
    )


def solve_rows(gram_matrix, panel):
    factor_low = jnp.linalg.cholesky(gram_matrix)
    return lax.linalg.triangular_solve(
        factor_low, panel, left_side=False, lower=True, transpose_a=True
    )


def reduced_basis(partial_value):
    summed = lax.psum(partial_value.astype(jnp.bfloat16), "ctr").astype(jnp.float32)
    return solve_rows(gram_of(summed), summed).astype(jnp.bfloat16)


def reduced_weights(partial_value):
    return lax.psum(partial_value.astype(jnp.bfloat16), "ctr")


def local_any(left_factor, left_inner, right_inner, right_outer, pattern, start_matrix):
    rows_here = left_factor.shape[0]
    tile_len = left_factor.shape[1]
    columns_here = left_factor.shape[2]
    rank_len = start_matrix.shape[1]
    blocks = columns_here // rank_len
    inner_piece = lax.all_gather(right_inner, "row", axis=0, tiled=True)
    outer_piece = lax.all_gather(right_outer, "row", axis=0, tiled=True)
    taken = inner_piece.shape[0]
    coupled = jnp.einsum(
        "itkr,tks->ikrs",
        left_inner.reshape(rows_here, taken, blocks, rank_len),
        inner_piece.reshape(taken, blocks, rank_len),
        preferred_element_type=jnp.float32,
    )
    coupled, outer_full = (coupled, outer_piece)
    coupled = (coupled * pattern.astype(jnp.float32)[:, :, None, None]).astype(jnp.bfloat16)
    inner_block = lax.optimization_barrier(coupled).astype(jnp.float32)

    def forward(vectors):
        shrunk = jnp.einsum(
            "tc,itq->icq", outer_full, vectors, preferred_element_type=jnp.float32
        ).reshape(rows_here, blocks, rank_len, rank_len)
        mapped = jnp.einsum("ikrs,iksq->ikrq", inner_block, shrunk, precision=highest)
        mapped = mapped.astype(jnp.bfloat16).reshape(rows_here, columns_here, rank_len)
        return jnp.einsum("itc,icq->itq", left_factor, mapped, preferred_element_type=jnp.float32)

    def adjoint(vectors):
        shrunk = jnp.einsum(
            "itc,itq->icq", left_factor, vectors, preferred_element_type=jnp.float32
        ).reshape(rows_here, blocks, rank_len, rank_len)
        mapped = jnp.einsum("ikrs,ikrq->iksq", inner_block, shrunk, precision=highest)
        mapped = mapped.astype(jnp.bfloat16).reshape(rows_here, columns_here, rank_len)
        return jnp.einsum("tc,icq->itq", outer_full, mapped, preferred_element_type=jnp.float32)

    start_bf = jnp.broadcast_to(
        start_matrix.astype(jnp.bfloat16)[None], (rows_here, tile_len, rank_len)
    )
    basis_now = reduced_basis(forward(start_bf))
    for sweep_index in range(STEPS):
        dual_basis = reduced_basis(adjoint(basis_now))
        basis_now = reduced_basis(forward(dual_basis))
    weights = reduced_weights(adjoint(basis_now))
    compressed_left = (basis_now.astype(jnp.float32) * math.sqrt(tile_len)).astype(jnp.bfloat16)
    return (compressed_left, weights)


F32 = jnp.float32
BF16 = jnp.bfloat16


def nn(a, b):
    return lax.dot_general(a, b, (((1,), (0,)), ((), ())), preferred_element_type=F32)


def nt(a, b):
    return lax.dot_general(a, b, (((1,), (1,)), ((), ())), preferred_element_type=F32)


def inverse_factor(gram):
    n = gram.shape[0]
    row_at = lax.broadcasted_iota(jnp.int32, (n, n), 0)
    col_at = lax.broadcasted_iota(jnp.int32, (n, n), 1)
    rest = gram
    inverse = jnp.where(row_at == col_at, 1.0, 0.0).astype(F32)
    scale = jnp.zeros_like(gram)
    for first in range(0, n, 8):
        last = min(first + 8, n)
        panel = {j: jnp.broadcast_to(rest[:, j : j + 1], (n, n)) for j in range(first, last)}
        for j in range(first, last):
            pivot = panel[j][j : j + 1, :]
            scale = jnp.where(row_at == j, lax.rsqrt(pivot), scale)
            ratio = jnp.where(row_at > j, panel[j] * (1.0 / pivot), 0.0)
            for m in range(j + 1, last):
                panel[m] = panel[m] - ratio * panel[m][j : j + 1, :]
            rest = rest - ratio * rest[j : j + 1, :]
            inverse = inverse - ratio * inverse[j : j + 1, :]
    return inverse * scale


def split(value):
    high = value.astype(BF16)
    return high, (value - high.astype(F32)).astype(BF16)


def apply_to(inverse, high):
    inverse_high, inverse_low = split(inverse)
    return nn(inverse_high, high) + nn(inverse_low, high)


def apply_wide(inverse, value):
    inverse_high, inverse_low = split(inverse)
    high, low = split(value)
    return nn(inverse_high, high) + nn(inverse_low, high) + nn(inverse_high, low)


def kernel(
    n_row, n_ctr, chunks,
    u_hbm, v_hbm, x_hbm, y_hbm, pattern_hbm, start_hbm,
    left_ref, right_ref,
    u_all, v_all, x_all, y_all, yb_all, c_all, z_ref, couple_out, couple_in, pattern_ref, start_ref, panels_ref, inverses_ref,
    local_sem, u_send, u_recv, x_send, x_recv, yz_send, yz_recv, yr_send, yr_recv,
    k_send, k_recv, l_send, l_recv, r_send, r_recv, i_send, i_recv,
):
    me_r, me_c = lax.axis_index("row"), lax.axis_index("ctr")
    tile = u_hbm.shape[1]
    cols = u_hbm.shape[2]
    part = x_hbm.shape[0]
    rank = start_ref.shape[0]
    blocks = pattern_ref.shape[1]
    step = tile // chunks
    z_peers = [lax.rem(me_c + d, n_ctr) for d in range(n_ctr)]
    r_peers = [lax.rem(me_r + d, n_row) for d in range(n_row)]
    mine = pl.ds(pl.multiple_of(me_r * part, part), part)

    def remote(src, dst, send, recv, where):
        return pltpu.make_async_remote_copy(
            src_ref=src, dst_ref=dst, send_sem=send, recv_sem=recv,
            device_id=where, device_id_type=pl.DeviceIdType.MESH,
        )

    v_copy = pltpu.make_async_copy(v_hbm, v_all, local_sem.at[0])
    v_copy.start()
    own_u = pltpu.make_async_copy(u_hbm.at[me_c], u_all.at[:, pl.ds(0, cols)], local_sem.at[1])
    own_u.start()
    own_x = pltpu.make_async_copy(x_hbm, x_all.at[mine, :], local_sem.at[2])
    own_y = pltpu.make_async_copy(y_hbm, y_all.at[mine, pl.ds(0, cols)], local_sem.at[3])
    get_pattern = pltpu.make_async_copy(pattern_hbm, pattern_ref, local_sem.at[4])
    get_start = pltpu.make_async_copy(start_hbm, start_ref, local_sem.at[5])
    for copy in (own_x, own_y, get_pattern, get_start):
        copy.start()

    barrier = pltpu.get_barrier_semaphore()
    for d in range(1, n_ctr):
        pl.semaphore_signal(barrier, inc=1, device_id={"ctr": z_peers[d]}, device_id_type=pl.DeviceIdType.MESH)
    for d in range(1, n_row):
        pl.semaphore_signal(barrier, inc=1, device_id={"row": r_peers[d]}, device_id_type=pl.DeviceIdType.MESH)
    pl.semaphore_wait(barrier, n_ctr + n_row - 2)

    yz = [None] + [
        remote(y_hbm, y_all.at[mine, pl.ds(d * cols, cols)], yz_send.at[d], yz_recv.at[d], {"ctr": z_peers[d]})
        for d in range(1, n_ctr)
    ]
    xs = [None] + [
        remote(x_hbm, x_all.at[mine, :], x_send.at[d], x_recv.at[d], {"row": r_peers[d]})
        for d in range(1, n_row)
    ]
    for copy in yz[1:] + xs[1:]:
        copy.start()
    us = {}
    for chunk in range(chunks):
        rows = pl.ds(chunk * step, step)
        for d in range(1, n_ctr):
            us[chunk, d] = remote(
                u_hbm.at[z_peers[d], rows, :], u_all.at[rows, pl.ds(d * cols, cols)],
                u_send.at[chunk, d], u_recv.at[chunk, d], {"ctr": z_peers[d]},
            )
            us[chunk, d].start()
    own_y.wait()
    yr = {}
    for k in range(n_ctr):
        if k:
            yz[k].wait_recv()
        for d in range(1, n_row):
            place = y_all.at[mine, pl.ds(k * cols, cols)]
            yr[k, d] = remote(
                place, place, yr_send.at[k, d], yr_recv.at[k, d], {"row": r_peers[d]}
            )
            yr[k, d].start()

    row_at = lax.broadcasted_iota(jnp.int32, (cols, cols), 0)
    col_at = lax.broadcasted_iota(jnp.int32, (cols, cols), 1)
    diagonal = jnp.where(row_at // rank == col_at // rank, 1.0, 0.0).astype(F32)
    fold = jnp.where(
        lax.broadcasted_iota(jnp.int32, (rank, cols), 1) % rank
        == lax.broadcasted_iota(jnp.int32, (rank, cols), 0), 1.0, 0.0
    ).astype(BF16)
    unfold = jnp.where(
        lax.broadcasted_iota(jnp.int32, (cols, rank), 0) % rank
        == lax.broadcasted_iota(jnp.int32, (cols, rank), 1), 1.0, 0.0
    ).astype(BF16)
    spread = jnp.where(
        lax.broadcasted_iota(jnp.int32, (blocks, cols), 1) // rank
        == lax.broadcasted_iota(jnp.int32, (blocks, cols), 0), 1.0, 0.0
    ).astype(F32)
    v_copy.wait()
    own_x.wait()
    get_pattern.wait()
    get_start.wait()
    for d in range(1, n_row):
        xs[d].wait_recv()
    x_turned = x_all[...].T
    couples = [None]
    for d in range(n_ctr):
        kept = pattern_ref[pl.ds(z_peers[d], 1), :].astype(F32)
        kept = nn(jnp.broadcast_to(kept, (8, blocks)).astype(BF16), spread.astype(BF16))[0:1, :]
        product = nn(x_turned, v_all[z_peers[d]])
        product = (product * diagonal * kept).astype(BF16)
        compact = nn(fold, product).astype(BF16)
        if d:
            couple_out[d] = compact
            copy = remote(couple_out.at[d], couple_in.at[d], k_send.at[d], k_recv.at[d], {"ctr": z_peers[d]})
            copy.start()
            couples.append(copy)
        else:
            couple_in[0] = compact

    for k in range(n_ctr):
        for d in range(1, n_row):
            yr[k, d].wait_recv()
        if k:
            couples[k].wait_recv()
        wide = (nn(unfold, couple_in[k]) * diagonal).astype(BF16)
        at = pl.ds(k * cols, cols)
        yb_all[:, at] = nn(y_all[:, at], wide).astype(BF16)

    own_u.wait()
    start = start_ref[...].astype(F32).astype(BF16)
    for chunk in range(chunks):
        rows = pl.ds(chunk * step, step)
        for d in range(1, n_ctr):
            us[chunk, d].wait_recv()
        c_all[rows, :] = nt(u_all[rows, :], yb_all[...]).astype(BF16)
        z_ref[:, rows] = nt(start, c_all[rows, :])

    panel = z_ref[...].astype(BF16)
    for sweep_index in range(STEPS):
        inverse = inverse_factor(nt(panel, panel))
        panel = apply_wide(inverse, nn(panel, c_all[...])).astype(BF16)
        inverse = inverse_factor(nt(panel, panel))
        panel = apply_wide(inverse, nt(panel, c_all[...])).astype(BF16)

    def share(ref, send, recv):
        copies = [
            remote(ref.at[me_c], ref.at[me_c], send.at[d], recv.at[d], {"ctr": z_peers[d]})
            for d in range(1, n_ctr)
        ]
        for copy in copies:
            copy.start()
        return copies

    panels_ref[me_c] = panel
    panel_copies = share(panels_ref, l_send, l_recv)
    inverse = inverse_factor(nt(panel, panel))
    inverses_ref[me_c] = inverse
    inverse_copies = share(inverses_ref, i_send, i_recv)
    right_ref[me_c] = apply_wide(inverse, nn(panel, c_all[...])).astype(BF16)
    right_copies = share(right_ref, r_send, r_recv)
    for d in range(n_ctr):
        if d:
            panel_copies[d - 1].wait_recv()
            inverse_copies[d - 1].wait_recv()
        source = lax.rem(me_c + (n_ctr - d), n_ctr)
        basis = apply_to(inverses_ref[source], panels_ref[source])
        left_ref[source] = (basis * math.sqrt(tile)).astype(BF16)
    for copy in right_copies:
        copy.wait_recv()
    for copy in panel_copies + inverse_copies + right_copies:
        copy.wait_send()
    for copy in yz[1:] + xs[1:] + list(us.values()) + list(yr.values()) + couples[1:]:
        copy.wait_send()


def local_tile(n_row, n_ctr, left_factor, left_inner, right_inner, right_outer, pattern, start_matrix):
    rows_here, tile, cols = left_factor.shape
    rank = start_matrix.shape[1]
    chunks = 4
    dma = lambda *shape: pltpu.SemaphoreType.DMA(shape)
    vmem = pl.BlockSpec(memory_space=pltpu.VMEM)
    hbm = pl.BlockSpec(memory_space=pl.ANY)
    width = n_ctr * cols
    turned = jax.ShapeDtypeStruct((rows_here, rank, tile), BF16)
    left, right = pl.pallas_call(
        functools.partial(kernel, n_row, n_ctr, chunks),
        out_shape=(turned, turned),
        in_specs=[hbm] * 6,
        out_specs=(vmem, vmem),
        scratch_shapes=[
            pltpu.VMEM((tile, width), BF16),
            pltpu.VMEM((rows_here, tile, cols), BF16),
            pltpu.VMEM((tile, cols), BF16),
            pltpu.VMEM((tile, width), BF16),
            pltpu.VMEM((tile, width), BF16),
            pltpu.VMEM((tile, tile), BF16),
            pltpu.VMEM((rank, tile), F32),
            pltpu.VMEM((n_ctr, rank, cols), BF16),
            pltpu.VMEM((n_ctr, rank, cols), BF16),
            pltpu.VMEM(pattern.shape, pattern.dtype),
            pltpu.VMEM((rank, tile), start_matrix.dtype),
            pltpu.VMEM((n_ctr, rank, tile), BF16),
            pltpu.VMEM((n_ctr, rank, rank), F32),
            dma(6),
            dma(chunks, n_ctr), dma(chunks, n_ctr),
            dma(n_row), dma(n_row),
            dma(n_ctr), dma(n_ctr),
            dma(n_ctr, n_row), dma(n_ctr, n_row),
            dma(n_ctr), dma(n_ctr),
            dma(n_ctr), dma(n_ctr),
            dma(n_ctr), dma(n_ctr),
            dma(n_ctr), dma(n_ctr),
        ],
        compiler_params=pltpu.CompilerParams(
            collective_id=0, has_side_effects=True, vmem_limit_bytes=62 * 1024 * 1024
        ),
    )(left_factor, left_inner, right_inner, right_outer, pattern, start_matrix.T)
    return left.transpose(0, 2, 1), right.transpose(0, 2, 1)


def solution(mesh):
    n_row, n_ctr = mesh.shape["row"], mesh.shape["ctr"]

    def local(left_factor, *others):
        if left_factor.shape[0] == n_ctr:
            return local_tile(n_row, n_ctr, left_factor, *others)
        return local_any(left_factor, *others)

    return jax.shard_map(
        local,
        mesh=mesh,
        in_specs=(
            P("row", None, "ctr"),
            P("row", None, "ctr"),
            P("row", "ctr"),
            P("row", "ctr"),
            P("row", "ctr"),
            P(),
        ),
        out_specs=(P("row", None, None), P("row", None, None)),
        check_vma=False,
    )
```

```python
import functools
import math

import jax
import jax.numpy as jnp
from jax import lax
from jax.experimental import pallas as pl
from jax.experimental.pallas import tpu as pltpu
from jax.sharding import PartitionSpec as P

STEPS = 2


highest = lax.Precision.HIGHEST


def gram_of(panel):
    return jnp.einsum(
        "itr,its->irs", panel, panel, precision=highest, preferred_element_type=jnp.float32
    )


def solve_rows(gram_matrix, panel):
    factor_low = jnp.linalg.cholesky(gram_matrix)
    return lax.linalg.triangular_solve(
        factor_low, panel, left_side=False, lower=True, transpose_a=True
    )


def reduced_basis(partial_value):
    summed = lax.psum(partial_value.astype(jnp.bfloat16), "ctr").astype(jnp.float32)
    return solve_rows(gram_of(summed), summed).astype(jnp.bfloat16)


def reduced_weights(partial_value):
    return lax.psum(partial_value.astype(jnp.bfloat16), "ctr")


def local_any(left_factor, left_inner, right_inner, right_outer, pattern, start_matrix):
    rows_here = left_factor.shape[0]
    tile_len = left_factor.shape[1]
    columns_here = left_factor.shape[2]
    rank_len = start_matrix.shape[1]
    blocks = columns_here // rank_len
    inner_piece = lax.all_gather(right_inner, "row", axis=0, tiled=True)
    outer_piece = lax.all_gather(right_outer, "row", axis=0, tiled=True)
    taken = inner_piece.shape[0]
    coupled = jnp.einsum(
        "itkr,tks->ikrs",
        left_inner.reshape(rows_here, taken, blocks, rank_len),
        inner_piece.reshape(taken, blocks, rank_len),
        preferred_element_type=jnp.float32,
    )
    coupled, outer_full = (coupled, outer_piece)
    coupled = (coupled * pattern.astype(jnp.float32)[:, :, None, None]).astype(jnp.bfloat16)
    inner_block = lax.optimization_barrier(coupled).astype(jnp.float32)

    def forward(vectors):
        shrunk = jnp.einsum(
            "tc,itq->icq", outer_full, vectors, preferred_element_type=jnp.float32
        ).reshape(rows_here, blocks, rank_len, rank_len)
        mapped = jnp.einsum("ikrs,iksq->ikrq", inner_block, shrunk, precision=highest)
        mapped = mapped.astype(jnp.bfloat16).reshape(rows_here, columns_here, rank_len)
        return jnp.einsum("itc,icq->itq", left_factor, mapped, preferred_element_type=jnp.float32)

    def adjoint(vectors):
        shrunk = jnp.einsum(
            "itc,itq->icq", left_factor, vectors, preferred_element_type=jnp.float32
        ).reshape(rows_here, blocks, rank_len, rank_len)
        mapped = jnp.einsum("ikrs,ikrq->iksq", inner_block, shrunk, precision=highest)
        mapped = mapped.astype(jnp.bfloat16).reshape(rows_here, columns_here, rank_len)
        return jnp.einsum("tc,icq->itq", outer_full, mapped, preferred_element_type=jnp.float32)

    start_bf = jnp.broadcast_to(
        start_matrix.astype(jnp.bfloat16)[None], (rows_here, tile_len, rank_len)
    )
    basis_now = reduced_basis(forward(start_bf))
    for sweep_index in range(STEPS):
        dual_basis = reduced_basis(adjoint(basis_now))
        basis_now = reduced_basis(forward(dual_basis))
    weights = reduced_weights(adjoint(basis_now))
    compressed_left = (basis_now.astype(jnp.float32) * math.sqrt(tile_len)).astype(jnp.bfloat16)
    return (compressed_left, weights)


F32 = jnp.float32
BF16 = jnp.bfloat16


def nn(a, b):
    return lax.dot_general(a, b, (((1,), (0,)), ((), ())), preferred_element_type=F32)


def nt(a, b):
    return lax.dot_general(a, b, (((1,), (1,)), ((), ())), preferred_element_type=F32)


def inverse_factor(gram):
    n = gram.shape[0]
    row_at = lax.broadcasted_iota(jnp.int32, (n, n), 0)
    col_at = lax.broadcasted_iota(jnp.int32, (n, n), 1)
    rest = gram
    inverse = jnp.where(row_at == col_at, 1.0, 0.0).astype(F32)
    scale = jnp.zeros_like(gram)
    for first in range(0, n, 8):
        last = min(first + 8, n)
        panel = {j: jnp.broadcast_to(rest[:, j : j + 1], (n, n)) for j in range(first, last)}
        for j in range(first, last):
            pivot = panel[j][j : j + 1, :]
            scale = jnp.where(row_at == j, lax.rsqrt(pivot), scale)
            ratio = jnp.where(row_at > j, panel[j] * (1.0 / pivot), 0.0)
            for m in range(j + 1, last):
                panel[m] = panel[m] - ratio * panel[m][j : j + 1, :]
            rest = rest - ratio * rest[j : j + 1, :]
            inverse = inverse - ratio * inverse[j : j + 1, :]
    return inverse * scale


def split(value):
    high = value.astype(BF16)
    return high, (value - high.astype(F32)).astype(BF16)


def apply_to(inverse, high):
    inverse_high, inverse_low = split(inverse)
    return nn(inverse_high, high) + nn(inverse_low, high)


def apply_wide(inverse, value):
    inverse_high, inverse_low = split(inverse)
    high, low = split(value)
    return nn(inverse_high, high) + nn(inverse_low, high) + nn(inverse_high, low)


def kernel(
    n_row, n_ctr, chunks,
    u_hbm, v_hbm, x_hbm, y_hbm, pattern_hbm, start_hbm,
    left_ref, right_ref,
    u_all, v_all, x_all, y_all, yb_all, c_all, z_ref, couple_out, couple_in, pattern_ref, start_ref,
    local_sem, u_send, u_recv, x_send, x_recv, yz_send, yz_recv, yr_send, yr_recv,
    k_send, k_recv, l_send, l_recv, r_send, r_recv,
):
    me_r, me_c = lax.axis_index("row"), lax.axis_index("ctr")
    tile = u_hbm.shape[1]
    cols = u_hbm.shape[2]
    part = x_hbm.shape[0]
    rank = start_ref.shape[0]
    blocks = pattern_ref.shape[1]
    step = tile // chunks
    z_peers = [lax.rem(me_c + d, n_ctr) for d in range(n_ctr)]
    r_peers = [lax.rem(me_r + d, n_row) for d in range(n_row)]
    mine = pl.ds(pl.multiple_of(me_r * part, part), part)

    def remote(src, dst, send, recv, where):
        return pltpu.make_async_remote_copy(
            src_ref=src, dst_ref=dst, send_sem=send, recv_sem=recv,
            device_id=where, device_id_type=pl.DeviceIdType.MESH,
        )

    v_copy = pltpu.make_async_copy(v_hbm, v_all, local_sem.at[0])
    v_copy.start()
    own_u = pltpu.make_async_copy(u_hbm.at[me_c], u_all.at[:, pl.ds(0, cols)], local_sem.at[1])
    own_u.start()
    own_x = pltpu.make_async_copy(x_hbm, x_all.at[mine, :], local_sem.at[2])
    own_y = pltpu.make_async_copy(y_hbm, y_all.at[mine, pl.ds(0, cols)], local_sem.at[3])
    get_pattern = pltpu.make_async_copy(pattern_hbm, pattern_ref, local_sem.at[4])
    get_start = pltpu.make_async_copy(start_hbm, start_ref, local_sem.at[5])
    for copy in (own_x, own_y, get_pattern, get_start):
        copy.start()

    barrier = pltpu.get_barrier_semaphore()
    for d in range(1, n_ctr):
        pl.semaphore_signal(barrier, inc=1, device_id={"ctr": z_peers[d]}, device_id_type=pl.DeviceIdType.MESH)
    for d in range(1, n_row):
        pl.semaphore_signal(barrier, inc=1, device_id={"row": r_peers[d]}, device_id_type=pl.DeviceIdType.MESH)
    pl.semaphore_wait(barrier, n_ctr + n_row - 2)

    def slot(at):
        return y_all.at[mine, pl.ds(at * cols, cols)]

    def hop_right(src, dst, send, recv, d):
        return remote(src, dst, send.at[0, d], recv.at[0, d + 1], {"ctr": me_c + 1})

    def hop_left(src, dst, send, recv, d):
        return remote(src, dst, send.at[1, d], recv.at[1, d + 1], {"ctr": me_c - 1})

    has_right, has_left = me_c + 1 < n_ctr, me_c > 0

    yz = [None] + [
        remote(y_hbm, y_all.at[mine, pl.ds(d * cols, cols)], yz_send.at[d], yz_recv.at[d], {"ctr": z_peers[d]})
        for d in range(1, n_ctr)
    ]
    xs = [None] + [
        remote(x_hbm, x_all.at[mine, :], x_send.at[d], x_recv.at[d], {"row": r_peers[d]})
        for d in range(1, n_row)
    ]
    for copy in yz[1:] + xs[1:]:
        copy.start()
    us = {}
    for chunk in range(chunks):
        rows = pl.ds(chunk * step, step)
        for d in range(1, n_ctr):
            us[chunk, d] = remote(
                u_hbm.at[z_peers[d], rows, :], u_all.at[rows, pl.ds(d * cols, cols)],
                u_send.at[chunk, d], u_recv.at[chunk, d], {"ctr": z_peers[d]},
            )
            us[chunk, d].start()
    own_y.wait()
    yr = {
        (k, d): remote(slot(k), slot(k), yr_send.at[k, d], yr_recv.at[k, d], {"row": r_peers[d]})
        for k in range(n_ctr)
        for d in range(1, n_row)
    }

    def to_rows(k):
        for d in range(1, n_row):
            yr[k, d].start()

    for k in range(n_ctr):
        if k:
            yz[k].wait_recv()
        to_rows(k)

    row_at = lax.broadcasted_iota(jnp.int32, (cols, cols), 0)
    col_at = lax.broadcasted_iota(jnp.int32, (cols, cols), 1)
    diagonal = jnp.where(row_at // rank == col_at // rank, 1.0, 0.0).astype(F32)
    fold = jnp.where(
        lax.broadcasted_iota(jnp.int32, (rank, cols), 1) % rank
        == lax.broadcasted_iota(jnp.int32, (rank, cols), 0), 1.0, 0.0
    ).astype(BF16)
    unfold = jnp.where(
        lax.broadcasted_iota(jnp.int32, (cols, rank), 0) % rank
        == lax.broadcasted_iota(jnp.int32, (cols, rank), 1), 1.0, 0.0
    ).astype(BF16)
    spread = jnp.where(
        lax.broadcasted_iota(jnp.int32, (blocks, cols), 1) // rank
        == lax.broadcasted_iota(jnp.int32, (blocks, cols), 0), 1.0, 0.0
    ).astype(F32)
    v_copy.wait()
    own_x.wait()
    get_pattern.wait()
    get_start.wait()
    for d in range(1, n_row):
        xs[d].wait_recv()
    x_turned = x_all[...].T
    couples = [None]
    for d in range(n_ctr):
        kept = pattern_ref[pl.ds(z_peers[d], 1), :].astype(F32)
        kept = nn(jnp.broadcast_to(kept, (8, blocks)).astype(BF16), spread.astype(BF16))[0:1, :]
        product = nn(x_turned, v_all[z_peers[d]])
        product = (product * diagonal * kept).astype(BF16)
        compact = nn(fold, product).astype(BF16)
        if d:
            couple_out[d] = compact
            copy = remote(couple_out.at[d], couple_in.at[d], k_send.at[d], k_recv.at[d], {"ctr": z_peers[d]})
            copy.start()
            couples.append(copy)
        else:
            couple_in[0] = compact

    for k in range(n_ctr):
        for d in range(1, n_row):
            yr[k, d].wait_recv()
        if k:
            couples[k].wait_recv()
        wide = (nn(unfold, couple_in[k]) * diagonal).astype(BF16)
        at = pl.ds(k * cols, cols)
        yb_all[:, at] = nn(y_all[:, at], wide).astype(BF16)

    own_u.wait()
    start = start_ref[...].astype(F32).astype(BF16)
    for chunk in range(chunks):
        rows = pl.ds(chunk * step, step)
        for d in range(1, n_ctr):
            us[chunk, d].wait_recv()
        c_all[rows, :] = nt(u_all[rows, :], yb_all[...]).astype(BF16)
        z_ref[:, rows] = nt(start, c_all[rows, :])

    panel = z_ref[...].astype(BF16)
    for sweep_index in range(STEPS):
        inverse = inverse_factor(nt(panel, panel))
        panel = apply_wide(inverse, nn(panel, c_all[...])).astype(BF16)
        inverse = inverse_factor(nt(panel, panel))
        panel = apply_wide(inverse, nt(panel, c_all[...])).astype(BF16)

    def out_right(ref, send, recv, d):
        at = ref.at[me_c - d]
        return hop_right(at, at, send, recv, d)

    def out_left(ref, send, recv, d):
        at = ref.at[me_c + d]
        return hop_left(at, at, send, recv, d)

    def begin(out):
        pl.when(has_right)(lambda: out_right(*out, 0).start())
        pl.when(has_left)(lambda: out_left(*out, 0).start())

    outs = [(left_ref, l_send, l_recv), (right_ref, r_send, r_recv)]
    inverse = inverse_factor(nt(panel, panel))
    left_ref[me_c] = (apply_to(inverse, panel) * math.sqrt(tile)).astype(BF16)
    begin(outs[0])
    right_ref[me_c] = apply_wide(inverse, nn(panel, c_all[...])).astype(BF16)
    begin(outs[1])
    for d in range(1, n_ctr):
        for out in outs:

            @pl.when(me_c >= d)
            def _():
                hop_right(out[0].at[me_c - d], out[0].at[me_c - d], out[1], out[2], d - 1).wait_recv()
                if d + 1 < n_ctr:
                    pl.when(has_right)(lambda: out_right(*out, d).start())

            @pl.when(me_c + d < n_ctr)
            def _():
                hop_left(out[0].at[me_c + d], out[0].at[me_c + d], out[1], out[2], d - 1).wait_recv()
                if d + 1 < n_ctr:
                    pl.when(has_left)(lambda: out_left(*out, d).start())

    for d in range(n_ctr - 1):

        @pl.when(jnp.logical_and(has_right, me_c >= d))
        def _():
            for out in outs:
                out_right(*out, d).wait_send()

        @pl.when(jnp.logical_and(has_left, me_c + d < n_ctr))
        def _():
            for out in outs:
                out_left(*out, d).wait_send()

    for copy in yz[1:] + xs[1:] + list(us.values()) + list(yr.values()) + couples[1:]:
        copy.wait_send()


def local_tile(n_row, n_ctr, left_factor, left_inner, right_inner, right_outer, pattern, start_matrix):
    rows_here, tile, cols = left_factor.shape
    rank = start_matrix.shape[1]
    chunks = 2
    dma = lambda *shape: pltpu.SemaphoreType.DMA(shape)
    vmem = pl.BlockSpec(memory_space=pltpu.VMEM)
    hbm = pl.BlockSpec(memory_space=pl.ANY)
    width = n_ctr * cols
    turned = jax.ShapeDtypeStruct((rows_here, rank, tile), BF16)
    left, right = pl.pallas_call(
        functools.partial(kernel, n_row, n_ctr, chunks),
        out_shape=(turned, turned),
        in_specs=[hbm] * 6,
        out_specs=(vmem, vmem),
        scratch_shapes=[
            pltpu.VMEM((tile, width), BF16),
            pltpu.VMEM((rows_here, tile, cols), BF16),
            pltpu.VMEM((tile, cols), BF16),
            pltpu.VMEM((tile, width), BF16),
            pltpu.VMEM((tile, width), BF16),
            pltpu.VMEM((tile, tile), BF16),
            pltpu.VMEM((rank, tile), F32),
            pltpu.VMEM((n_ctr, rank, cols), BF16),
            pltpu.VMEM((n_ctr, rank, cols), BF16),
            pltpu.VMEM(pattern.shape, pattern.dtype),
            pltpu.VMEM((rank, tile), start_matrix.dtype),
            dma(6),
            dma(chunks, n_ctr), dma(chunks, n_ctr),
            dma(n_row), dma(n_row),
            dma(n_ctr), dma(n_ctr),
            dma(n_ctr, n_row), dma(n_ctr, n_row),
            dma(n_ctr), dma(n_ctr),
            dma(2, n_ctr), dma(2, n_ctr),
            dma(2, n_ctr), dma(2, n_ctr),
        ],
        compiler_params=pltpu.CompilerParams(
            collective_id=0, has_side_effects=True, vmem_limit_bytes=62 * 1024 * 1024
        ),
    )(left_factor, left_inner, right_inner, right_outer, pattern, start_matrix.T)
    return left.transpose(0, 2, 1), right.transpose(0, 2, 1)


def solution(mesh):
    n_row, n_ctr = mesh.shape["row"], mesh.shape["ctr"]

    def local(left_factor, *others):
        if left_factor.shape[0] == n_ctr:
            return local_tile(n_row, n_ctr, left_factor, *others)
        return local_any(left_factor, *others)

    return jax.shard_map(
        local,
        mesh=mesh,
        in_specs=(
            P("row", None, "ctr"),
            P("row", None, "ctr"),
            P("row", "ctr"),
            P("row", "ctr"),
            P("row", "ctr"),
            P(),
        ),
        out_specs=(P("row", None, None), P("row", None, None)),
        check_vma=False,
    )
```

```python
import functools
import math

import jax
import jax.numpy as jnp
from jax import lax
from jax.experimental import pallas as pl
from jax.experimental.pallas import tpu as pltpu
from jax.sharding import PartitionSpec as P

STEPS = 2


highest = lax.Precision.HIGHEST


def gram_of(panel):
    return jnp.einsum(
        "itr,its->irs", panel, panel, precision=highest, preferred_element_type=jnp.float32
    )


def solve_rows(gram_matrix, panel):
    factor_low = jnp.linalg.cholesky(gram_matrix)
    return lax.linalg.triangular_solve(
        factor_low, panel, left_side=False, lower=True, transpose_a=True
    )


def reduced_basis(partial_value):
    summed = lax.psum(partial_value.astype(jnp.bfloat16), "ctr").astype(jnp.float32)
    return solve_rows(gram_of(summed), summed).astype(jnp.bfloat16)


def reduced_weights(partial_value):
    return lax.psum(partial_value.astype(jnp.bfloat16), "ctr")


def local_any(left_factor, left_inner, right_inner, right_outer, pattern, start_matrix):
    rows_here = left_factor.shape[0]
    tile_len = left_factor.shape[1]
    columns_here = left_factor.shape[2]
    rank_len = start_matrix.shape[1]
    blocks = columns_here // rank_len
    inner_piece = lax.all_gather(right_inner, "row", axis=0, tiled=True)
    outer_piece = lax.all_gather(right_outer, "row", axis=0, tiled=True)
    taken = inner_piece.shape[0]
    coupled = jnp.einsum(
        "itkr,tks->ikrs",
        left_inner.reshape(rows_here, taken, blocks, rank_len),
        inner_piece.reshape(taken, blocks, rank_len),
        preferred_element_type=jnp.float32,
    )
    coupled, outer_full = (coupled, outer_piece)
    coupled = (coupled * pattern.astype(jnp.float32)[:, :, None, None]).astype(jnp.bfloat16)
    inner_block = lax.optimization_barrier(coupled).astype(jnp.float32)

    def forward(vectors):
        shrunk = jnp.einsum(
            "tc,itq->icq", outer_full, vectors, preferred_element_type=jnp.float32
        ).reshape(rows_here, blocks, rank_len, rank_len)
        mapped = jnp.einsum("ikrs,iksq->ikrq", inner_block, shrunk, precision=highest)
        mapped = mapped.astype(jnp.bfloat16).reshape(rows_here, columns_here, rank_len)
        return jnp.einsum("itc,icq->itq", left_factor, mapped, preferred_element_type=jnp.float32)

    def adjoint(vectors):
        shrunk = jnp.einsum(
            "itc,itq->icq", left_factor, vectors, preferred_element_type=jnp.float32
        ).reshape(rows_here, blocks, rank_len, rank_len)
        mapped = jnp.einsum("ikrs,ikrq->iksq", inner_block, shrunk, precision=highest)
        mapped = mapped.astype(jnp.bfloat16).reshape(rows_here, columns_here, rank_len)
        return jnp.einsum("tc,icq->itq", outer_full, mapped, preferred_element_type=jnp.float32)

    start_bf = jnp.broadcast_to(
        start_matrix.astype(jnp.bfloat16)[None], (rows_here, tile_len, rank_len)
    )
    basis_now = reduced_basis(forward(start_bf))
    for sweep_index in range(STEPS):
        dual_basis = reduced_basis(adjoint(basis_now))
        basis_now = reduced_basis(forward(dual_basis))
    weights = reduced_weights(adjoint(basis_now))
    compressed_left = (basis_now.astype(jnp.float32) * math.sqrt(tile_len)).astype(jnp.bfloat16)
    return (compressed_left, weights)


F32 = jnp.float32
BF16 = jnp.bfloat16


def nn(a, b):
    return lax.dot_general(a, b, (((1,), (0,)), ((), ())), preferred_element_type=F32)


def nt(a, b):
    return lax.dot_general(a, b, (((1,), (1,)), ((), ())), preferred_element_type=F32)


def inverse_factor(gram):
    n = gram.shape[0]
    row_at = lax.broadcasted_iota(jnp.int32, (n, n), 0)
    col_at = lax.broadcasted_iota(jnp.int32, (n, n), 1)
    rest = gram
    inverse = jnp.where(row_at == col_at, 1.0, 0.0).astype(F32)
    scale = jnp.zeros_like(gram)
    for first in range(0, n, 8):
        last = min(first + 8, n)
        panel = {j: jnp.broadcast_to(rest[:, j : j + 1], (n, n)) for j in range(first, last)}
        for j in range(first, last):
            pivot = panel[j][j : j + 1, :]
            scale = jnp.where(row_at == j, lax.rsqrt(pivot), scale)
            ratio = jnp.where(row_at > j, panel[j] * (1.0 / pivot), 0.0)
            for m in range(j + 1, last):
                panel[m] = panel[m] - ratio * panel[m][j : j + 1, :]
            rest = rest - ratio * rest[j : j + 1, :]
            inverse = inverse - ratio * inverse[j : j + 1, :]
    return inverse * scale


def split(value):
    high = value.astype(BF16)
    return high, (value - high.astype(F32)).astype(BF16)


def apply_to(inverse, high):
    inverse_high, inverse_low = split(inverse)
    return nn(inverse_high, high) + nn(inverse_low, high)


def apply_wide(inverse, value):
    inverse_high, inverse_low = split(inverse)
    high, low = split(value)
    return nn(inverse_high, high) + nn(inverse_low, high) + nn(inverse_high, low)


def kernel(
    n_row, n_ctr, chunks,
    u_hbm, v_hbm, x_hbm, y_hbm, pattern_hbm, start_hbm,
    left_ref, right_ref,
    u_all, v_all, x_all, y_all, yb_all, c_all, z_ref, couple_out, couple_in, pattern_ref, start_ref,
    local_sem, u_send, u_recv, x_send, x_recv, yz_send, yz_recv, yr_send, yr_recv,
    k_send, k_recv, l_send, l_recv, r_send, r_recv,
):
    me_r, me_c = lax.axis_index("row"), lax.axis_index("ctr")
    tile = u_hbm.shape[1]
    cols = u_hbm.shape[2]
    part = x_hbm.shape[0]
    rank = start_ref.shape[0]
    blocks = pattern_ref.shape[1]
    step = tile // chunks
    z_peers = [lax.rem(me_c + d, n_ctr) for d in range(n_ctr)]
    r_peers = [lax.rem(me_r + d, n_row) for d in range(n_row)]
    mine = pl.ds(pl.multiple_of(me_r * part, part), part)

    def remote(src, dst, send, recv, where):
        return pltpu.make_async_remote_copy(
            src_ref=src, dst_ref=dst, send_sem=send, recv_sem=recv,
            device_id=where, device_id_type=pl.DeviceIdType.MESH,
        )

    v_copy = pltpu.make_async_copy(v_hbm, v_all, local_sem.at[0])
    v_copy.start()
    own_u = pltpu.make_async_copy(u_hbm.at[me_c], u_all.at[:, pl.ds(0, cols)], local_sem.at[1])
    own_u.start()
    own_x = pltpu.make_async_copy(x_hbm, x_all.at[mine, :], local_sem.at[2])
    own_y = pltpu.make_async_copy(y_hbm, y_all.at[mine, pl.ds(0, cols)], local_sem.at[3])
    get_pattern = pltpu.make_async_copy(pattern_hbm, pattern_ref, local_sem.at[4])
    get_start = pltpu.make_async_copy(start_hbm, start_ref, local_sem.at[5])
    for copy in (own_x, own_y, get_pattern, get_start):
        copy.start()

    barrier = pltpu.get_barrier_semaphore()
    for d in range(1, n_ctr):
        pl.semaphore_signal(barrier, inc=1, device_id={"ctr": z_peers[d]}, device_id_type=pl.DeviceIdType.MESH)
    for d in range(1, n_row):
        pl.semaphore_signal(barrier, inc=1, device_id={"row": r_peers[d]}, device_id_type=pl.DeviceIdType.MESH)
    pl.semaphore_wait(barrier, n_ctr + n_row - 2)

    def slot(at):
        return y_all.at[mine, pl.ds(at * cols, cols)]

    def hop_right(src, dst, send, recv, d):
        return remote(src, dst, send.at[0, d], recv.at[0, d + 1], {"ctr": me_c + 1})

    def hop_left(src, dst, send, recv, d):
        return remote(src, dst, send.at[1, d], recv.at[1, d + 1], {"ctr": me_c - 1})

    has_right, has_left = me_c + 1 < n_ctr, me_c > 0

    yz = [None] + [
        remote(y_hbm, y_all.at[mine, pl.ds(d * cols, cols)], yz_send.at[d], yz_recv.at[d], {"ctr": z_peers[d]})
        for d in range(1, n_ctr)
    ]
    xs = [None] + [
        remote(x_hbm, x_all.at[mine, :], x_send.at[d], x_recv.at[d], {"row": r_peers[d]})
        for d in range(1, n_row)
    ]
    for copy in yz[1:] + xs[1:]:
        copy.start()
    us = {}
    for chunk in range(chunks):
        rows = pl.ds(chunk * step, step)
        for d in range(1, n_ctr):
            us[chunk, d] = remote(
                u_hbm.at[z_peers[d], rows, :], u_all.at[rows, pl.ds(d * cols, cols)],
                u_send.at[chunk, d], u_recv.at[chunk, d], {"ctr": z_peers[d]},
            )
            if chunk == 0:
                us[chunk, d].start()
    own_y.wait()
    yr = {
        (k, d): remote(slot(k), slot(k), yr_send.at[k, d], yr_recv.at[k, d], {"row": r_peers[d]})
        for k in range(n_ctr)
        for d in range(1, n_row)
    }

    def to_rows(k):
        for d in range(1, n_row):
            yr[k, d].start()

    for k in range(n_ctr):
        if k:
            yz[k].wait_recv()
        to_rows(k)

    row_at = lax.broadcasted_iota(jnp.int32, (cols, cols), 0)
    col_at = lax.broadcasted_iota(jnp.int32, (cols, cols), 1)
    diagonal = jnp.where(row_at // rank == col_at // rank, 1.0, 0.0).astype(F32)
    fold = jnp.where(
        lax.broadcasted_iota(jnp.int32, (rank, cols), 1) % rank
        == lax.broadcasted_iota(jnp.int32, (rank, cols), 0), 1.0, 0.0
    ).astype(BF16)
    unfold = jnp.where(
        lax.broadcasted_iota(jnp.int32, (cols, rank), 0) % rank
        == lax.broadcasted_iota(jnp.int32, (cols, rank), 1), 1.0, 0.0
    ).astype(BF16)
    spread = jnp.where(
        lax.broadcasted_iota(jnp.int32, (blocks, cols), 1) // rank
        == lax.broadcasted_iota(jnp.int32, (blocks, cols), 0), 1.0, 0.0
    ).astype(F32)
    v_copy.wait()
    own_x.wait()
    get_pattern.wait()
    get_start.wait()
    for d in range(1, n_row):
        xs[d].wait_recv()
    x_turned = x_all[...].T
    couples = [None]
    for d in range(n_ctr):
        kept = pattern_ref[pl.ds(z_peers[d], 1), :].astype(F32)
        kept = nn(jnp.broadcast_to(kept, (8, blocks)).astype(BF16), spread.astype(BF16))[0:1, :]
        product = nn(x_turned, v_all[z_peers[d]])
        product = (product * diagonal * kept).astype(BF16)
        compact = nn(fold, product).astype(BF16)
        if d:
            couple_out[d] = compact
            copy = remote(couple_out.at[d], couple_in.at[d], k_send.at[d], k_recv.at[d], {"ctr": z_peers[d]})
            copy.start()
            couples.append(copy)
        else:
            couple_in[0] = compact

    for chunk in range(1, chunks):
        for d in range(1, n_ctr):
            us[chunk, d].start()

    for k in range(n_ctr):
        for d in range(1, n_row):
            yr[k, d].wait_recv()
        if k:
            couples[k].wait_recv()
        wide = (nn(unfold, couple_in[k]) * diagonal).astype(BF16)
        at = pl.ds(k * cols, cols)
        yb_all[:, at] = nn(y_all[:, at], wide).astype(BF16)

    own_u.wait()
    start = start_ref[...].astype(F32).astype(BF16)
    for chunk in range(chunks):
        rows = pl.ds(chunk * step, step)
        for d in range(1, n_ctr):
            us[chunk, d].wait_recv()
        c_all[rows, :] = nt(u_all[rows, :], yb_all[...]).astype(BF16)
        z_ref[:, rows] = nt(start, c_all[rows, :])

    panel = z_ref[...].astype(BF16)
    for sweep_index in range(STEPS):
        inverse = inverse_factor(nt(panel, panel))
        panel = apply_wide(inverse, nn(panel, c_all[...])).astype(BF16)
        inverse = inverse_factor(nt(panel, panel))
        panel = apply_wide(inverse, nt(panel, c_all[...])).astype(BF16)

    def out_right(ref, send, recv, d):
        at = ref.at[me_c - d]
        return hop_right(at, at, send, recv, d)

    def out_left(ref, send, recv, d):
        at = ref.at[me_c + d]
        return hop_left(at, at, send, recv, d)

    def begin(out):
        pl.when(has_right)(lambda: out_right(*out, 0).start())
        pl.when(has_left)(lambda: out_left(*out, 0).start())

    outs = [(left_ref, l_send, l_recv), (right_ref, r_send, r_recv)]
    inverse = inverse_factor(nt(panel, panel))
    left_ref[me_c] = (apply_to(inverse, panel) * math.sqrt(tile)).astype(BF16)
    begin(outs[0])
    right_ref[me_c] = apply_wide(inverse, nn(panel, c_all[...])).astype(BF16)
    begin(outs[1])
    for d in range(1, n_ctr):
        for out in outs:

            @pl.when(me_c >= d)
            def _():
                hop_right(out[0].at[me_c - d], out[0].at[me_c - d], out[1], out[2], d - 1).wait_recv()
                if d + 1 < n_ctr:
                    pl.when(has_right)(lambda: out_right(*out, d).start())

            @pl.when(me_c + d < n_ctr)
            def _():
                hop_left(out[0].at[me_c + d], out[0].at[me_c + d], out[1], out[2], d - 1).wait_recv()
                if d + 1 < n_ctr:
                    pl.when(has_left)(lambda: out_left(*out, d).start())

    for d in range(n_ctr - 1):

        @pl.when(jnp.logical_and(has_right, me_c >= d))
        def _():
            for out in outs:
                out_right(*out, d).wait_send()

        @pl.when(jnp.logical_and(has_left, me_c + d < n_ctr))
        def _():
            for out in outs:
                out_left(*out, d).wait_send()

    for copy in yz[1:] + xs[1:] + list(us.values()) + list(yr.values()) + couples[1:]:
        copy.wait_send()


def local_tile(n_row, n_ctr, left_factor, left_inner, right_inner, right_outer, pattern, start_matrix):
    rows_here, tile, cols = left_factor.shape
    rank = start_matrix.shape[1]
    chunks = 4
    dma = lambda *shape: pltpu.SemaphoreType.DMA(shape)
    vmem = pl.BlockSpec(memory_space=pltpu.VMEM)
    hbm = pl.BlockSpec(memory_space=pl.ANY)
    width = n_ctr * cols
    turned = jax.ShapeDtypeStruct((rows_here, rank, tile), BF16)
    left, right = pl.pallas_call(
        functools.partial(kernel, n_row, n_ctr, chunks),
        out_shape=(turned, turned),
        in_specs=[hbm] * 6,
        out_specs=(vmem, vmem),
        scratch_shapes=[
            pltpu.VMEM((tile, width), BF16),
            pltpu.VMEM((rows_here, tile, cols), BF16),
            pltpu.VMEM((tile, cols), BF16),
            pltpu.VMEM((tile, width), BF16),
            pltpu.VMEM((tile, width), BF16),
            pltpu.VMEM((tile, tile), BF16),
            pltpu.VMEM((rank, tile), F32),
            pltpu.VMEM((n_ctr, rank, cols), BF16),
            pltpu.VMEM((n_ctr, rank, cols), BF16),
            pltpu.VMEM(pattern.shape, pattern.dtype),
            pltpu.VMEM((rank, tile), start_matrix.dtype),
            dma(6),
            dma(chunks, n_ctr), dma(chunks, n_ctr),
            dma(n_row), dma(n_row),
            dma(n_ctr), dma(n_ctr),
            dma(n_ctr, n_row), dma(n_ctr, n_row),
            dma(n_ctr), dma(n_ctr),
            dma(2, n_ctr), dma(2, n_ctr),
            dma(2, n_ctr), dma(2, n_ctr),
        ],
        compiler_params=pltpu.CompilerParams(
            collective_id=0, has_side_effects=True, vmem_limit_bytes=62 * 1024 * 1024
        ),
    )(left_factor, left_inner, right_inner, right_outer, pattern, start_matrix.T)
    return left.transpose(0, 2, 1), right.transpose(0, 2, 1)


def solution(mesh):
    n_row, n_ctr = mesh.shape["row"], mesh.shape["ctr"]

    def local(left_factor, *others):
        if left_factor.shape[0] == n_ctr:
            return local_tile(n_row, n_ctr, left_factor, *others)
        return local_any(left_factor, *others)

    return jax.shard_map(
        local,
        mesh=mesh,
        in_specs=(
            P("row", None, "ctr"),
            P("row", None, "ctr"),
            P("row", "ctr"),
            P("row", "ctr"),
            P("row", "ctr"),
            P(),
        ),
        out_specs=(P("row", None, None), P("row", None, None)),
        check_vma=False,
    )
```
